32 devices in a mesh: grp: 4 (over y, core), tp: 2 (over x), seq: 4 (over z).
Axes of the slice: x: 2, y: 2, z: 4, core: 2. Of those that a mesh axis runs over, the one named last changes fastest.
Arguments:
- crops: bfloat16 [4, 4, 576, 1024], P('grp', 'seq', 'tp'), may hold values from -6 to 6
- dout: bfloat16 [4, 4, 576, 1024], P('grp', 'seq', None, 'tp'), may hold values from -0.796875 to 0.796875
- crop_count: int32 [4], P('grp'), may hold values from 2 to 4, as said below
- crop_ids: int32 [4, 4], P('grp'), may hold values from 0 to 3, each once within a row
- seq_slot: int32 [4, 4], P('grp'), may hold values from 0 to 3, as said below
- norm_gain: bfloat16 [1024], replicated, may hold values from 0.099609375 to 1.8984375
- qkv_weight: bfloat16 [3, 1024, 1024], P(None, None, 'tp'), may hold values from -40 to 40
Outputs:
- weight_grad: float32 [3072, 1024], P(('grp', 'seq'), 'tp')
The draws below stay inside these ranges and needn't reach their ends.
Inputs may be any that keep to these rules, and one draw needn't show every extreme that they name: `crop_count`: some page selects 4 crops. `seq_slot`: distinct within a row; only the first crop_count entries of a row are used. `crop_ids`: only the first crop_count entries of a row are used.
All inputs are finite; a program needn't handle non-finite values.
Results may differ from the reference program's by a relative error of at most 0.0084.
Values may be sent and summed in bfloat16 or wider, within the bound.
A program may use at most 64 MiB of HBM per device.

```python
import jax
import jax.numpy as jnp
from jax import lax

DV = 1024
HEADS = 16
HD = 64
CTOK = 576
SELMAX = 4
SLOTS = 4
PAGES = 4


def draw_crop_count(key, part):
    counts = jax.random.randint(key, (PAGES,), (SELMAX + 2) // 3, SELMAX + 1)
    full_page = jax.random.randint(jax.random.fold_in(key, 7), (), 0, PAGES)
    return jnp.where(jnp.arange(PAGES) == full_page, SELMAX, counts).astype(jnp.int32)


def slot_row(page_key):
    return jax.random.permutation(page_key, SLOTS)[:SELMAX]


def draw_seq_slot(key, part):
    page_keys = jax.random.split(jax.random.fold_in(key, 11), PAGES)
    return jax.vmap(slot_row)(page_keys).astype(jnp.int32)


def draw_qkv_weight(key, part):
    normal_part = jax.random.normal(key, (3, DV, HEADS * HD), jnp.float32) * DV ** (-0.5)
    normal_part = jnp.clip(normal_part, -1.0, 1.0)
    return normal_part.astype(jnp.bfloat16)


def level_of(rng, dims, pieces, low, top_value):
    def one(dim, parts):
        steps = jax.random.uniform(jax.random.fold_in(jax.random.fold_in(rng, 6), dim), (parts,), jnp.float32, low / len(pieces), top_value / len(pieces))
        return jnp.repeat(jnp.exp(steps), dims[dim] // parts).reshape((-1,) + (1,) * (len(dims) - dim - 1))

    loudness = one(*pieces[0])
    for cut in pieces[1:]:
        loudness = loudness * one(*cut)
    return loudness


def normal_values(rng, dims, scale, bound, pieces=(), kind=jnp.bfloat16):
    loudness = level_of(rng, dims, pieces, -0.22, 0.18) if pieces else 1.0
    entries = jax.random.normal(rng, dims, jnp.float32) * scale * loudness
    return jnp.minimum(jnp.maximum(entries, -bound), bound).astype(kind)


def setup_inputs(seed: int = 0) -> dict:
    streams_of = jax.random.split(jax.random.key(seed), 8)
    return {
        "crops": normal_values(streams_of[0], (PAGES, SELMAX, CTOK, DV), 1.0, 6.0, ((0, 4), (1, 4), (2, 2))),
        "dout": normal_values(streams_of[1], (PAGES, SLOTS, CTOK, HEADS * HD), 0.1, 0.796875, ((0, 4), (1, 4), (3, 2))),
        "crop_count": draw_crop_count(jax.random.fold_in(streams_of[7], 71), 0),
        "crop_ids": jax.vmap(lambda own: jax.random.permutation(own, SELMAX))(jax.random.split(streams_of[3], PAGES)).reshape((PAGES, SELMAX)).astype(jnp.int32),
        "seq_slot": draw_seq_slot(jax.random.fold_in(streams_of[7], 71), 0),
        "norm_gain": jnp.clip(1.0 + 0.18 * jax.random.normal(streams_of[5], (DV,), jnp.float32), 0.099609375, 1.8984375).astype(jnp.bfloat16),
        "qkv_weight": draw_qkv_weight(jax.random.fold_in(streams_of[7], 71), 0),
    }


def crop_grads(inputs, cotangent, norm_gain, weight):
    crops_here, tok_count, head_cols = cotangent.shape
    head_count = head_cols // HD
    values = inputs.astype(jnp.float32)
    centred = values - lax.optimization_barrier(jnp.mean(values, axis=-1, keepdims=True))
    spread = lax.optimization_barrier(jnp.mean(centred * centred, axis=-1, keepdims=True))
    normed = (centred * lax.rsqrt(spread + 1e-05) * norm_gain.astype(jnp.float32)).astype(jnp.bfloat16)
    projected = jnp.einsum('etd,cdw->cetw', normed.astype(jnp.float32), weight.astype(jnp.float32)).astype(jnp.bfloat16)
    heads_view = projected.reshape(3, crops_here, tok_count, head_count, HD)
    queries = heads_view[0].astype(jnp.float32)
    key_rows = heads_view[1].astype(jnp.float32)
    value_rows = heads_view[2].astype(jnp.float32)
    score_scale = HD ** (-0.5)
    scores = jnp.einsum('eqhd,ekhd->ehqk', queries, key_rows) * score_scale
    attention = jax.nn.softmax(scores, axis=-1)
    attention_low = attention.astype(jnp.bfloat16).astype(jnp.float32)
    upstream = cotangent.reshape(crops_here, tok_count, head_count, HD).astype(jnp.float32)
    grad_values = jnp.einsum('ehqk,eqhd->ekhd', attention_low, upstream).astype(jnp.bfloat16)
    grad_attention = jnp.einsum('eqhd,ekhd->ehqk', upstream, value_rows)
    grad_scores = attention * (grad_attention - lax.optimization_barrier(jnp.sum(attention * grad_attention, axis=-1, keepdims=True)))
    scaled = (grad_scores * score_scale).astype(jnp.bfloat16).astype(jnp.float32)
    grad_queries = jnp.einsum('ehqk,ekhd->eqhd', scaled, key_rows).astype(jnp.bfloat16)
    grad_keys = jnp.einsum('ehqk,eqhd->ekhd', scaled, queries).astype(jnp.bfloat16)
    stacked = jnp.stack([grad_queries, grad_keys, grad_values]).reshape(3, crops_here, tok_count, head_cols)
    return jnp.einsum('etd,cetw->cdw', normed.astype(jnp.float32), stacked.astype(jnp.float32))

def reference(crops, dout, crop_count, crop_ids, seq_slot, norm_gain, qkv_weight):
    most_crops = crop_ids.shape[1]
    page_total = crops.shape[0]
    head_cols = dout.shape[3]

    def accumulate(running, position):
        page_no = (position // most_crops).astype(jnp.int32)
        rank_no = (position % most_crops).astype(jnp.int32)
        is_live = rank_no < crop_count[page_no]
        candidate = crop_ids[page_no, rank_no].astype(jnp.int32)
        slot_no = seq_slot[page_no, rank_no].astype(jnp.int32)
        inputs = crops[page_no, candidate][None]
        cotangent = dout[page_no, slot_no][None]
        local_grad = crop_grads(inputs, cotangent, norm_gain, qkv_weight)
        return (running + jnp.where(is_live, local_grad, jnp.zeros_like(local_grad)), None)
    start_grad = jnp.zeros((3, crops.shape[3], head_cols), jnp.float32)
    running, _ = lax.scan(accumulate, start_grad, jnp.arange(page_total * most_crops, dtype=jnp.int32))
    return running.reshape(3 * crops.shape[3], head_cols)
```

```python
import functools

import jax
import jax.numpy as jnp
from jax import lax
from jax.experimental import pallas as pl
from jax.experimental.pallas import tpu as pltpu
from jax.sharding import PartitionSpec as P

HD = 64
LANES = 128
MESH = pl.DeviceIdType.MESH
LOG2E = 1.4426950408889634
F32 = jnp.float32
BF16 = jnp.bfloat16


def mm(a, b, ca, cb):
    return lax.dot_general(a, b, (((ca,), (cb,)), ((), ())), preferred_element_type=F32)


def kernel(
    sizes,
    x_ref,
    g_ref,
    count_ref,
    ids_ref,
    slot_ref,
    gain_ref,
    w_hbm,
    out_ref,
    w_ref,
    x_all,
    normed32,
    normed,
    normed_t,
    proj,
    g_all,
    total,
    acc,
    s1,
    r1,
    s2,
    r2,
    s3,
    r3,
    w_sem,
    xs_sem,
    xr_sem,
    gs_sem,
    gr_sem,
    s1_sem,
    r1_sem,
    s2_sem,
    r2_sem,
    s3_sem,
    r3_sem,
):
    n_grp, n_tp, n_seq, n_core = sizes
    n_y = n_grp // n_core
    grp = lax.axis_index("grp")
    tp = lax.axis_index("tp")
    seq = lax.axis_index("seq")
    y = grp // n_core
    core = grp % n_core
    other = n_core - 1 - core
    groups = proj.shape[1]
    tokens = proj.shape[2]
    width = w_ref.shape[1]
    pieces, piece_rows = x_all.shape[1], x_all.shape[2]
    out_rows = out_ref.shape[0]
    block_rows = n_seq * out_rows
    hops = n_seq - 1

    def at(g=None, t=None, s=None):
        return (grp if g is None else g, tp if t is None else t, seq if s is None else s)

    partners = [at(t=(tp + d) % n_tp) for d in range(1, n_tp)]
    partners += [at(s=(seq + d) % n_seq) for d in range(1, n_seq)]
    partners += [at(g=((y + d) % n_y) * n_core + core) for d in range(1, n_y)]
    if n_core > 1:
        partners += [at(g=y * n_core + other)]

    w_copy = pltpu.make_async_copy(w_hbm, w_ref, w_sem)
    w_copy.start()
    barrier = pltpu.get_barrier_semaphore()
    for partner in partners:
        pl.semaphore_signal(barrier, inc=1, device_id=partner, device_id_type=MESH)
    pl.semaphore_wait(barrier, len(partners))

    def x_copy(d, piece):
        return pltpu.make_async_remote_copy(
            src_ref=x_ref.at[piece],
            dst_ref=x_all.at[d, piece],
            send_sem=xs_sem.at[d - 1, piece],
            recv_sem=xr_sem.at[d - 1, piece],
            device_id=at(t=(tp + n_tp - d) % n_tp),
            device_id_type=MESH,
        )

    for piece in range(pieces):
        for d in range(1, n_tp):
            x_copy(d, piece).start()

    def g_copy(way, hop, group):
        step = 1 if way == 0 else -1
        block = seq - step * hop
        return pltpu.make_async_remote_copy(
            src_ref=g_all.at[block, group],
            dst_ref=g_all.at[block, group],
            send_sem=gs_sem.at[way, hop, group],
            recv_sem=gr_sem.at[way, hop, group],
            device_id=at(s=seq + step),
            device_id_type=MESH,
        )

    def g_wait_copy(way, hop, group):
        step = 1 if way == 0 else -1
        block = seq - step * (hop + 1)
        return pltpu.make_async_remote_copy(
            src_ref=g_all.at[block, group],
            dst_ref=g_all.at[block, group],
            send_sem=gs_sem.at[way, hop, group],
            recv_sem=gr_sem.at[way, hop, group],
            device_id=at(s=seq - step),
            device_id_type=MESH,
        )

    def sends(way, hop):
        if way == 0:
            return (seq >= hop) & (seq + 1 < n_seq)
        return (seq + hop < n_seq) & (seq >= 1)

    def receives(way, hop):
        return seq >= hop + 1 if way == 0 else seq + hop + 1 < n_seq

    def g_level(level):
        for way in range(2):

            @pl.when((level < groups) & sends(way, 0))
            def _():
                g_copy(way, 0, level).start()

        for hop in range(hops - 1, -1, -1):
            group = level - 1 - hop
            inside = (group >= 0) & (group < groups)
            for way in range(2):

                @pl.when(inside & receives(way, hop))
                def _():
                    g_wait_copy(way, hop, group).wait_recv()

                if hop + 1 < hops:

                    @pl.when(inside & sends(way, hop + 1))
                    def _():
                        g_copy(way, hop + 1, group).start()

    for group in range(groups):
        g_all[seq, group] = g_ref[:, group * LANES : (group + 1) * LANES]
    g_level(0)

    gain = gain_ref[...].astype(F32)
    aligned = piece_rows % 16 == 0

    def norm_piece(owner, piece, values):
        values = values.astype(F32)
        centred = values - jnp.mean(values, axis=-1, keepdims=True)
        spread = jnp.mean(centred * centred, axis=-1, keepdims=True)
        result = centred * lax.rsqrt(spread + 1e-05) * gain
        place = owner * pieces + piece
        if aligned:
            start = pl.multiple_of(place * piece_rows, 16)
            normed[pl.ds(start, piece_rows), :] = result.astype(BF16)
        else:
            normed32[place] = result

    for piece in range(pieces):
        norm_piece(tp, piece, x_ref[piece])
    for level in range(1, hops):
        g_level(level)
    for piece in range(pieces):
        for d in range(1, n_tp):
            x_copy(d, piece).wait_recv()
            norm_piece((tp + d) % n_tp, piece, x_all[d, piece])
    if not aligned:
        normed[...] = normed32[...].reshape(tokens, width).astype(BF16)

    w_copy.wait()
    for c in range(3):
        for group in range(groups):
            columns = slice(group * LANES, (group + 1) * LANES)
            proj[c, group] = mm(normed[...], w_ref[c, :, columns], 1, 0).astype(BF16)
    normed_t[...] = normed[...].T

    source = jnp.int32(0)
    live = jnp.int32(0)
    for rank in range(ids_ref.shape[1]):
        match = (ids_ref[0, rank] == seq) & (rank < count_ref[0])
        source = jnp.where(match, slot_ref[0, rank], source)
        live = jnp.where(match, 1, live)
    picks = [jnp.where(source == block, live, 0).astype(F32) for block in range(n_seq)]

    lane = lax.broadcasted_iota(jnp.int32, (1, LANES), 1)
    heads_here = LANES // HD
    masks = [
        ((lane >= h * HD) & (lane < (h + 1) * HD)).astype(F32).astype(BF16)
        for h in range(heads_here)
    ]

    def head(group, mask, cotangent):
        queries = proj[0, group]
        keys_own = proj[1, group] * mask
        values_own = proj[2, group] * mask
        scores = mm(keys_own, queries, 1, 1) * (HD**-0.5 * LOG2E)
        powers = jnp.exp2(scores - jnp.max(scores, axis=0, keepdims=True))
        attention = powers * (1.0 / jnp.sum(powers, axis=0, keepdims=True))
        grad_values = mm(attention.astype(BF16), cotangent * mask, 1, 0)
        grad_attention = mm(values_own, cotangent, 1, 1)
        weighted = attention * grad_attention
        inner = jnp.sum(weighted, axis=0, keepdims=True)
        scaled = ((weighted - attention * inner) * HD**-0.5).astype(BF16)
        grad_queries = mm(scaled, keys_own, 0, 0)
        grad_keys = mm(scaled, queries * mask, 1, 0)
        return grad_queries, grad_keys, grad_values

    def rows_of(who):
        return pl.ds(pl.multiple_of(who * block_rows, block_rows), block_rows)

    def copy1(group):
        return pltpu.make_async_remote_copy(
            src_ref=s1.at[group],
            dst_ref=r1.at[group],
            send_sem=s1_sem.at[group],
            recv_sem=r1_sem.at[group],
            device_id=at(g=y * n_core + other),
            device_id_type=MESH,
        )

    def copy2(group, d):
        return pltpu.make_async_remote_copy(
            src_ref=s2.at[group, d - 1],
            dst_ref=r2.at[group, d - 1],
            send_sem=s2_sem.at[group, d - 1],
            recv_sem=r2_sem.at[group, d - 1],
            device_id=at(g=((y + d) % n_y) * n_core + core),
            device_id_type=MESH,
        )

    def copy3(group, d):
        return pltpu.make_async_remote_copy(
            src_ref=s3.at[group, d - 1],
            dst_ref=r3.at[group, d - 1],
            send_sem=s3_sem.at[group, d - 1],
            recv_sem=r3_sem.at[group, d - 1],
            device_id=at(s=(seq + d) % n_seq),
            device_id_type=MESH,
        )

    def reduce1(group):
        if n_core > 1:
            for place in range(n_y):
                s1[group, place] = total[group, rows_of(place * n_core + other), :].astype(BF16)
            copy1(group).start()

    def reduce2(group):
        if n_core > 1:
            copy1(group).wait_recv()

        def part(place):
            mine = total[group, rows_of(place * n_core + core), :]
            return mine + r1[group, place].astype(F32) if n_core > 1 else mine

        for d in range(1, n_y):
            s2[group, d - 1] = part((y + d) % n_y).astype(BF16)
            copy2(group, d).start()
        acc[group] = part(y)

    def reduce3(group):
        for d in range(1, n_y):
            copy2(group, d).wait_recv()

        def part(place):
            rows = pl.ds(pl.multiple_of(place * out_rows, out_rows), out_rows)
            value = acc[group, rows, :]
            for d in range(1, n_y):
                value = value + r2[group, d - 1, rows, :].astype(F32)
            return value

        for d in range(1, n_seq):
            s3[group, d - 1] = part((seq + d) % n_seq).astype(BF16)
            copy3(group, d).start()
        acc[group, 0:out_rows, :] = part(seq)

    def reduce4(group):
        value = acc[group, 0:out_rows, :]
        for d in range(1, n_seq):
            copy3(group, d).wait_recv()
            value = value + r3[group, d - 1].astype(F32)
        return value

    def one_group(group, carry):
        g_level(hops + group)
        cotangent = g_all[0, group].astype(F32) * picks[0]
        for block in range(1, n_seq):
            cotangent = cotangent + g_all[block, group].astype(F32) * picks[block]
        cotangent = cotangent.astype(BF16)
        grads = head(group, masks[0], cotangent)

        @pl.when(group >= 1)
        def _():
            reduce2(group - 1)

        for mask in masks[1:]:
            more = head(group, mask, cotangent)
            grads = [a + b for a, b in zip(grads, more)]

        @pl.when(group >= 1)
        def _():
            reduce3(group - 1)

        joined = jnp.concatenate([grad.astype(BF16) for grad in grads], axis=1)
        product = mm(normed_t[...], joined, 1, 0)
        for c in range(3):
            total[group, c * width : (c + 1) * width, :] = product[:, c * LANES : (c + 1) * LANES]
        reduce1(group)
        return carry

    lax.fori_loop(0, groups, one_group, jnp.int32(0))
    reduce2(groups - 1)
    reduce3(groups - 1)
    for group in range(groups):
        out_ref[:, group * LANES : (group + 1) * LANES] = reduce4(group)

    for piece in range(pieces):
        for d in range(1, n_tp):
            x_copy(d, piece).wait_send()
    for hop in range(hops):
        for way in range(2):

            @pl.when(sends(way, hop))
            def _():
                for group in range(groups):
                    g_copy(way, hop, group).wait_send()

    for group in range(groups):
        if n_core > 1:
            copy1(group).wait_send()
        for d in range(1, n_y):
            copy2(group, d).wait_send()
        for d in range(1, n_seq):
            copy3(group, d).wait_send()


def body(sizes, crops, dout, crop_count, crop_ids, seq_slot, norm_gain, qkv_weight):
    n_grp, n_tp, n_seq, n_core = sizes
    n_y = n_grp // n_core
    tok_local, width = crops.shape[2], crops.shape[3]
    tokens, cols = dout.shape[2], dout.shape[3]
    groups = cols // LANES
    out_rows = 3 * width // (n_grp * n_seq)
    block_rows = n_seq * out_rows
    pieces = 3 if tok_local % 48 == 0 else 1
    piece_rows = tok_local // pieces
    aligned = piece_rows % 16 == 0
    hops = n_seq - 1
    vmem = pl.BlockSpec(memory_space=pltpu.VMEM)
    smem = pl.BlockSpec(memory_space=pltpu.SMEM)
    dma = pltpu.SemaphoreType.DMA
    scratch = [
        pltpu.VMEM((3, width, cols), BF16),
        pltpu.VMEM((n_tp, pieces, piece_rows, width), BF16),
        pltpu.VMEM((8, LANES) if aligned else (n_tp * pieces, piece_rows, width), F32),
        pltpu.VMEM((tokens, width), BF16),
        pltpu.VMEM((width, tokens), BF16),
        pltpu.VMEM((3, groups, tokens, LANES), BF16),
        pltpu.VMEM((n_seq, groups, tokens, LANES), BF16),
        pltpu.VMEM((groups, 3 * width, LANES), F32),
        pltpu.VMEM((groups, block_rows, LANES), F32),
        pltpu.VMEM((groups, n_y, block_rows, LANES), BF16),
        pltpu.VMEM((groups, n_y, block_rows, LANES), BF16),
        pltpu.VMEM((groups, max(n_y - 1, 1), block_rows, LANES), BF16),
        pltpu.VMEM((groups, max(n_y - 1, 1), block_rows, LANES), BF16),
        pltpu.VMEM((groups, max(n_seq - 1, 1), out_rows, LANES), BF16),
        pltpu.VMEM((groups, max(n_seq - 1, 1), out_rows, LANES), BF16),
        dma,
        dma((max(n_tp - 1, 1), pieces)),
        dma((max(n_tp - 1, 1), pieces)),
        dma((2, hops, groups)),
        dma((2, hops, groups)),
        dma((groups,)),
        dma((groups,)),
        dma((groups, max(n_y - 1, 1))),
        dma((groups, max(n_y - 1, 1))),
        dma((groups, n_seq - 1)),
        dma((groups, n_seq - 1)),
    ]
    return pl.pallas_call(
        functools.partial(kernel, sizes),
        out_shape=jax.ShapeDtypeStruct((out_rows, cols), F32),
        in_specs=[vmem, vmem, smem, smem, smem, vmem, pl.BlockSpec(memory_space=pl.ANY)],
        out_specs=vmem,
        scratch_shapes=scratch,
        compiler_params=pltpu.CompilerParams(
            collective_id=0, has_side_effects=True, vmem_limit_bytes=56 * 2**20
        ),
        cost_estimate=pl.CostEstimate(
            flops=22 * tokens * width * cols, bytes_accessed=8 * width * cols, transcendentals=0
        ),
    )(
        crops.reshape(pieces, piece_rows, width),
        dout.reshape(tokens, cols),
        crop_count,
        crop_ids,
        seq_slot,
        norm_gain.reshape(1, width),
        qkv_weight,
    )


def solution(mesh):
    n_grp, n_tp, n_seq = mesh.shape["grp"], mesh.shape["tp"], mesh.shape["seq"]
    n_core = 2 if n_grp % 2 == 0 else 1
    in_specs = (
        P("grp", "seq", "tp", None),
        P("grp", "seq", None, "tp"),
        P("grp"),
        P("grp", None),
        P("grp", None),
        P(),
        P(None, None, "tp"),
    )
    out_specs = P(("grp", "seq"), "tp")
    return jax.shard_map(
        functools.partial(body, (n_grp, n_tp, n_seq, n_core)),
        mesh=mesh,
        in_specs=in_specs,
        out_specs=out_specs,
        check_vma=False,
    )
```

```python
import functools

import jax
import jax.numpy as jnp
from jax import lax
from jax.experimental import pallas as pl
from jax.experimental.pallas import tpu as pltpu
from jax.sharding import PartitionSpec as P

HD = 64
LANES = 128
MESH = pl.DeviceIdType.MESH
LOG2E = 1.4426950408889634
F32 = jnp.float32
BF16 = jnp.bfloat16


def mm(a, b, ca, cb):
    return lax.dot_general(a, b, (((ca,), (cb,)), ((), ())), preferred_element_type=F32)


def kernel(
    sizes,
    x_ref,
    g_ref,
    count_ref,
    ids_ref,
    slot_ref,
    gain_ref,
    w_hbm,
    out_ref,
    w_ref,
    x_all,
    normed32,
    normed,
    normed_t,
    proj,
    g_all,
    picked,
    total,
    acc,
    s1,
    r1,
    s2,
    r2,
    s3,
    r3,
    w_sem,
    xs_sem,
    xr_sem,
    gs_sem,
    gr_sem,
    s1_sem,
    r1_sem,
    s2_sem,
    r2_sem,
    s3_sem,
    r3_sem,
):
    n_grp, n_tp, n_seq, n_core = sizes
    n_y = n_grp // n_core
    grp = lax.axis_index("grp")
    tp = lax.axis_index("tp")
    seq = lax.axis_index("seq")
    y = grp // n_core
    core = grp % n_core
    other = n_core - 1 - core
    groups = proj.shape[1]
    tokens = proj.shape[2]
    width = w_ref.shape[1]
    pieces, piece_rows = x_all.shape[1], x_all.shape[2]
    out_rows = out_ref.shape[0]
    block_rows = n_seq * out_rows
    hops = n_seq - 1

    def at(g=None, t=None, s=None):
        return (grp if g is None else g, tp if t is None else t, seq if s is None else s)

    partners = [at(t=(tp + d) % n_tp) for d in range(1, n_tp)]
    partners += [at(s=(seq + d) % n_seq) for d in range(1, n_seq)]
    partners += [at(g=((y + d) % n_y) * n_core + core) for d in range(1, n_y)]
    if n_core > 1:
        partners += [at(g=y * n_core + other)]

    w_copy = pltpu.make_async_copy(w_hbm, w_ref, w_sem)
    w_copy.start()
    barrier = pltpu.get_barrier_semaphore()
    for partner in partners:
        pl.semaphore_signal(barrier, inc=1, device_id=partner, device_id_type=MESH)
    pl.semaphore_wait(barrier, len(partners))

    def x_copy(d, piece):
        return pltpu.make_async_remote_copy(
            src_ref=x_ref.at[piece],
            dst_ref=x_all.at[d, piece],
            send_sem=xs_sem.at[d - 1, piece],
            recv_sem=xr_sem.at[d - 1, piece],
            device_id=at(t=(tp + n_tp - d) % n_tp),
            device_id_type=MESH,
        )

    for piece in range(pieces):
        for d in range(1, n_tp):
            x_copy(d, piece).start()

    def g_copy(way, hop, group):
        step = 1 if way == 0 else -1
        block = seq - step * hop
        return pltpu.make_async_remote_copy(
            src_ref=g_all.at[block, group],
            dst_ref=g_all.at[block, group],
            send_sem=gs_sem.at[way, hop, group],
            recv_sem=gr_sem.at[way, hop, group],
            device_id=at(s=seq + step),
            device_id_type=MESH,
        )

    def g_wait_copy(way, hop, group):
        step = 1 if way == 0 else -1
        block = seq - step * (hop + 1)
        return pltpu.make_async_remote_copy(
            src_ref=g_all.at[block, group],
            dst_ref=g_all.at[block, group],
            send_sem=gs_sem.at[way, hop, group],
            recv_sem=gr_sem.at[way, hop, group],
            device_id=at(s=seq - step),
            device_id_type=MESH,
        )

    def position(way):
        return seq if way == 0 else n_seq - 1 - seq

    def sends(way, hop):
        where = position(way)
        if hop == hops - 1:
            return where == n_seq - 2
        return (where >= hop) & (where <= n_seq - 3)

    def receives(way, hop):
        where = position(way)
        if hop == hops - 1:
            return where == n_seq - 1
        return (where >= hop + 1) & (where <= n_seq - 2)

    def picks_of(who):
        source = jnp.int32(0)
        live = jnp.int32(0)
        for rank in range(ids_ref.shape[1]):
            match = (ids_ref[0, rank] == who) & (rank < count_ref[0])
            source = jnp.where(match, slot_ref[0, rank], source)
            live = jnp.where(match, 1, live)
        return [jnp.where(source == block, live, 0).astype(F32) for block in range(n_seq)]

    end_picks = [picks_of(n_seq - 1), picks_of(0)]

    def pick_copy(way, group):
        step = 1 if way == 0 else -1
        return pltpu.make_async_remote_copy(
            src_ref=picked.at[way, group],
            dst_ref=g_all.at[seq, group],
            send_sem=gs_sem.at[way, hops - 1, group],
            recv_sem=gr_sem.at[way, hops - 1, group],
            device_id=at(s=seq + step),
            device_id_type=MESH,
        )

    def pick_wait_copy(way, group):
        step = 1 if way == 0 else -1
        return pltpu.make_async_remote_copy(
            src_ref=picked.at[way, group],
            dst_ref=g_all.at[seq - step, group],
            send_sem=gs_sem.at[way, hops - 1, group],
            recv_sem=gr_sem.at[way, hops - 1, group],
            device_id=at(s=seq - step),
            device_id_type=MESH,
        )

    def g_level(level):
        for way in range(2):

            @pl.when((level < groups) & sends(way, 0))
            def _():
                g_copy(way, 0, level).start()

        for hop in range(hops - 1, -1, -1):
            group = level - 1 - hop
            inside = (group >= 0) & (group < groups)
            for way in range(2):

                @pl.when(inside & receives(way, hop))
                def _():
                    if hop == hops - 1:
                        pick_wait_copy(way, group).wait_recv()
                    else:
                        g_wait_copy(way, hop, group).wait_recv()

                if hop + 1 < hops - 1:

                    @pl.when(inside & sends(way, hop + 1))
                    def _():
                        g_copy(way, hop + 1, group).start()

                if hop + 1 == hops - 1:

                    @pl.when(inside & sends(way, hop + 1))
                    def _():
                        blocks = range(n_seq - 1) if way == 0 else range(1, n_seq)
                        value = jnp.zeros((tokens, LANES), F32)
                        for block in blocks:
                            value = value + g_all[block, group].astype(F32) * end_picks[way][block]
                        picked[way, group] = value.astype(BF16)
                        pick_copy(way, group).start()

    for group in range(groups):
        g_all[seq, group] = g_ref[:, group * LANES : (group + 1) * LANES]
    for way in range(2):

        @pl.when(position(way) == n_seq - 1)
        def _():
            for block in range(n_seq - 2) if way == 0 else range(2, n_seq):
                g_all[block] = jnp.zeros(g_all.shape[1:], BF16)

    g_level(0)

    gain = gain_ref[...].astype(F32)
    aligned = piece_rows % 16 == 0

    def norm_piece(owner, piece, values):
        values = values.astype(F32)
        centred = values - jnp.mean(values, axis=-1, keepdims=True)
        spread = jnp.mean(centred * centred, axis=-1, keepdims=True)
        result = centred * lax.rsqrt(spread + 1e-05) * gain
        place = owner * pieces + piece
        if aligned:
            start = pl.multiple_of(place * piece_rows, 16)
            normed[pl.ds(start, piece_rows), :] = result.astype(BF16)
        else:
            normed32[place] = result

    for piece in range(pieces):
        norm_piece(tp, piece, x_ref[piece])
    for level in range(1, hops):
        g_level(level)
    w_copy.wait()

    def project(owner):
        rows = pl.ds(pl.multiple_of(owner * pieces * piece_rows, 16), pieces * piece_rows)
        for c in range(3):
            for group in range(groups):
                columns = slice(group * LANES, (group + 1) * LANES)
                result = mm(normed[rows, :], w_ref[c, :, columns], 1, 0)
                proj[c, group, rows, :] = result.astype(BF16)

    if aligned:
        project(tp)
    for piece in range(pieces):
        for d in range(1, n_tp):
            x_copy(d, piece).wait_recv()
            norm_piece((tp + d) % n_tp, piece, x_all[d, piece])
    if aligned:
        for d in range(1, n_tp):
            project((tp + d) % n_tp)
    else:
        normed[...] = normed32[...].reshape(tokens, width).astype(BF16)
        for c in range(3):
            for group in range(groups):
                columns = slice(group * LANES, (group + 1) * LANES)
                proj[c, group] = mm(normed[...], w_ref[c, :, columns], 1, 0).astype(BF16)
    normed_t[...] = normed[...].T

    picks = picks_of(seq)
    for block in range(n_seq):
        sent = ((seq == n_seq - 1) & (block == n_seq - 2)) | ((seq == 0) & (block == 1))
        picks[block] = jnp.where(sent, 1.0, picks[block])

    lane = lax.broadcasted_iota(jnp.int32, (1, LANES), 1)
    heads_here = LANES // HD
    masks = [
        ((lane >= h * HD) & (lane < (h + 1) * HD)).astype(F32).astype(BF16)
        for h in range(heads_here)
    ]

    def head(group, mask, cotangent):
        queries = proj[0, group]
        keys_own = proj[1, group] * mask
        values_own = proj[2, group] * mask
        scores = mm(keys_own, queries, 1, 1) * (HD**-0.5 * LOG2E)
        powers = jnp.exp2(scores - jnp.max(scores, axis=0, keepdims=True))
        attention = powers * (1.0 / jnp.sum(powers, axis=0, keepdims=True))
        grad_values = mm(attention.astype(BF16), cotangent * mask, 1, 0)
        grad_attention = mm(values_own, cotangent, 1, 1)
        weighted = attention * grad_attention
        inner = jnp.sum(weighted, axis=0, keepdims=True)
        scaled = ((weighted - attention * inner) * HD**-0.5).astype(BF16)
        grad_queries = mm(scaled, keys_own, 0, 0)
        grad_keys = mm(scaled, queries * mask, 1, 0)
        return grad_queries, grad_keys, grad_values

    def rows_of(who):
        return pl.ds(pl.multiple_of(who * block_rows, block_rows), block_rows)

    def copy1(group):
        return pltpu.make_async_remote_copy(
            src_ref=s1.at[group],
            dst_ref=r1.at[group],
            send_sem=s1_sem.at[group],
            recv_sem=r1_sem.at[group],
            device_id=at(g=y * n_core + other),
            device_id_type=MESH,
        )

    def copy2(group, d):
        return pltpu.make_async_remote_copy(
            src_ref=s2.at[group, d - 1],
            dst_ref=r2.at[group, d - 1],
            send_sem=s2_sem.at[group, d - 1],
            recv_sem=r2_sem.at[group, d - 1],
            device_id=at(g=((y + d) % n_y) * n_core + core),
            device_id_type=MESH,
        )

    def copy3(group, d):
        return pltpu.make_async_remote_copy(
            src_ref=s3.at[group, d - 1],
            dst_ref=r3.at[group, d - 1],
            send_sem=s3_sem.at[group, d - 1],
            recv_sem=r3_sem.at[group, d - 1],
            device_id=at(s=(seq + d) % n_seq),
            device_id_type=MESH,
        )

    def reduce1(group):
        if n_core > 1:
            for place in range(n_y):
                s1[group, place] = total[group, rows_of(place * n_core + other), :].astype(BF16)
            copy1(group).start()

    def reduce2(group):
        if n_core > 1:
            copy1(group).wait_recv()

        def part(place):
            mine = total[group, rows_of(place * n_core + core), :]
            return mine + r1[group, place].astype(F32) if n_core > 1 else mine

        for d in range(1, n_y):
            s2[group, d - 1] = part((y + d) % n_y).astype(BF16)
            copy2(group, d).start()
        acc[group] = part(y)

    def reduce3(group):
        for d in range(1, n_y):
            copy2(group, d).wait_recv()

        def part(place):
            rows = pl.ds(pl.multiple_of(place * out_rows, out_rows), out_rows)
            value = acc[group, rows, :]
            for d in range(1, n_y):
                value = value + r2[group, d - 1, rows, :].astype(F32)
            return value

        for d in range(1, n_seq):
            s3[group, d - 1] = part((seq + d) % n_seq).astype(BF16)
            copy3(group, d).start()
        acc[group, 0:out_rows, :] = part(seq)

    def reduce4(group):
        value = acc[group, 0:out_rows, :]
        for d in range(1, n_seq):
            copy3(group, d).wait_recv()
            value = value + r3[group, d - 1].astype(F32)
        return value

    def one_group(group, carry):
        g_level(hops + group)
        cotangent = g_all[0, group].astype(F32) * picks[0]
        for block in range(1, n_seq):
            cotangent = cotangent + g_all[block, group].astype(F32) * picks[block]
        cotangent = cotangent.astype(BF16)
        grads = head(group, masks[0], cotangent)

        @pl.when(group >= 1)
        def _():
            reduce2(group - 1)

        @pl.when(group >= 2)
        def _():
            reduce3(group - 2)

        for mask in masks[1:]:
            more = head(group, mask, cotangent)
            grads = [a + b for a, b in zip(grads, more)]

        joined = jnp.concatenate([grad.astype(BF16) for grad in grads], axis=1)
        product = mm(normed_t[...], joined, 1, 0)
        for c in range(3):
            total[group, c * width : (c + 1) * width, :] = product[:, c * LANES : (c + 1) * LANES]
        reduce1(group)
        return carry

    lax.fori_loop(0, groups, one_group, jnp.int32(0))
    reduce2(groups - 1)
    for group in range(max(groups - 2, 0), groups):
        reduce3(group)
    for group in range(groups):
        out_ref[:, group * LANES : (group + 1) * LANES] = reduce4(group)

    for piece in range(pieces):
        for d in range(1, n_tp):
            x_copy(d, piece).wait_send()
    for hop in range(hops):
        for way in range(2):

            @pl.when(sends(way, hop))
            def _():
                for group in range(groups):
                    copy = pick_copy(way, group) if hop == hops - 1 else g_copy(way, hop, group)
                    copy.wait_send()

    for group in range(groups):
        if n_core > 1:
            copy1(group).wait_send()
        for d in range(1, n_y):
            copy2(group, d).wait_send()
        for d in range(1, n_seq):
            copy3(group, d).wait_send()


def body(sizes, crops, dout, crop_count, crop_ids, seq_slot, norm_gain, qkv_weight):
    n_grp, n_tp, n_seq, n_core = sizes
    n_y = n_grp // n_core
    tok_local, width = crops.shape[2], crops.shape[3]
    tokens, cols = dout.shape[2], dout.shape[3]
    groups = cols // LANES
    out_rows = 3 * width // (n_grp * n_seq)
    block_rows = n_seq * out_rows
    pieces = 3 if tok_local % 48 == 0 else 1
    piece_rows = tok_local // pieces
    aligned = piece_rows % 16 == 0
    hops = n_seq - 1
    vmem = pl.BlockSpec(memory_space=pltpu.VMEM)
    smem = pl.BlockSpec(memory_space=pltpu.SMEM)
    dma = pltpu.SemaphoreType.DMA
    scratch = [
        pltpu.VMEM((3, width, cols), BF16),
        pltpu.VMEM((n_tp, pieces, piece_rows, width), BF16),
        pltpu.VMEM((8, LANES) if aligned else (n_tp * pieces, piece_rows, width), F32),
        pltpu.VMEM((tokens, width), BF16),
        pltpu.VMEM((width, tokens), BF16),
        pltpu.VMEM((3, groups, tokens, LANES), BF16),
        pltpu.VMEM((n_seq, groups, tokens, LANES), BF16),
        pltpu.VMEM((2, groups, tokens, LANES), BF16),
        pltpu.VMEM((groups, 3 * width, LANES), F32),
        pltpu.VMEM((groups, block_rows, LANES), F32),
        pltpu.VMEM((groups, n_y, block_rows, LANES), BF16),
        pltpu.VMEM((groups, n_y, block_rows, LANES), BF16),
        pltpu.VMEM((groups, max(n_y - 1, 1), block_rows, LANES), BF16),
        pltpu.VMEM((groups, max(n_y - 1, 1), block_rows, LANES), BF16),
        pltpu.VMEM((groups, max(n_seq - 1, 1), out_rows, LANES), BF16),
        pltpu.VMEM((groups, max(n_seq - 1, 1), out_rows, LANES), BF16),
        dma,
        dma((max(n_tp - 1, 1), pieces)),
        dma((max(n_tp - 1, 1), pieces)),
        dma((2, hops, groups)),
        dma((2, hops, groups)),
        dma((groups,)),
        dma((groups,)),
        dma((groups, max(n_y - 1, 1))),
        dma((groups, max(n_y - 1, 1))),
        dma((groups, n_seq - 1)),
        dma((groups, n_seq - 1)),
    ]
    return pl.pallas_call(
        functools.partial(kernel, sizes),
        out_shape=jax.ShapeDtypeStruct((out_rows, cols), F32),
        in_specs=[vmem, vmem, smem, smem, smem, vmem, pl.BlockSpec(memory_space=pl.ANY)],
        out_specs=vmem,
        scratch_shapes=scratch,
        compiler_params=pltpu.CompilerParams(
            collective_id=0, has_side_effects=True, vmem_limit_bytes=56 * 2**20
        ),
        cost_estimate=pl.CostEstimate(
            flops=22 * tokens * width * cols, bytes_accessed=8 * width * cols, transcendentals=0
        ),
    )(
        crops.reshape(pieces, piece_rows, width),
        dout.reshape(tokens, cols),
        crop_count,
        crop_ids,
        seq_slot,
        norm_gain.reshape(1, width),
        qkv_weight,
    )


def solution(mesh):
    n_grp, n_tp, n_seq = mesh.shape["grp"], mesh.shape["tp"], mesh.shape["seq"]
    n_core = 2 if n_grp % 2 == 0 else 1
    in_specs = (
        P("grp", "seq", "tp", None),
        P("grp", "seq", None, "tp"),
        P("grp"),
        P("grp", None),
        P("grp", None),
        P(),
        P(None, None, "tp"),
    )
    out_specs = P(("grp", "seq"), "tp")
    return jax.shard_map(
        functools.partial(body, (n_grp, n_tp, n_seq, n_core)),
        mesh=mesh,
        in_specs=in_specs,
        out_specs=out_specs,
        check_vma=False,
    )
```

```python
import functools

import jax
import jax.numpy as jnp
from jax import lax
from jax.experimental import pallas as pl
from jax.experimental.pallas import tpu as pltpu
from jax.sharding import PartitionSpec as P

HD = 64
LANES = 128
MESH = pl.DeviceIdType.MESH
LOG2E = 1.4426950408889634
F32 = jnp.float32
BF16 = jnp.bfloat16


def mm(a, b, ca, cb):
    return lax.dot_general(a, b, (((ca,), (cb,)), ((), ())), preferred_element_type=F32)


def kernel(
    sizes,
    x_ref,
    g_ref,
    count_ref,
    ids_ref,
    slot_ref,
    gain_ref,
    w_hbm,
    out_ref,
    w_ref,
    x_all,
    normed32,
    normed,
    normed_t,
    proj,
    g_all,
    picked,
    total,
    acc,
    own,
    s1,
    r1,
    s2,
    r2,
    s3,
    r3,
    w_sem,
    xs_sem,
    xr_sem,
    gs_sem,
    gr_sem,
    s1_sem,
    r1_sem,
    s2_sem,
    r2_sem,
    s3_sem,
    r3_sem,
):
    n_grp, n_tp, n_seq, n_core = sizes
    n_y = n_grp // n_core
    grp = lax.axis_index("grp")
    tp = lax.axis_index("tp")
    seq = lax.axis_index("seq")
    y = grp // n_core
    core = grp % n_core
    other = n_core - 1 - core
    groups = proj.shape[1]
    tokens = proj.shape[2]
    width = w_ref.shape[1]
    pieces, piece_rows = x_all.shape[1], x_all.shape[2]
    out_rows = out_ref.shape[0]
    block_rows = n_seq * out_rows
    hops = n_seq - 1

    def at(g=None, t=None, s=None):
        return (grp if g is None else g, tp if t is None else t, seq if s is None else s)

    partners = [at(t=(tp + d) % n_tp) for d in range(1, n_tp)]
    partners += [at(s=(seq + d) % n_seq) for d in range(1, n_seq)]
    partners += [at(g=((y + d) % n_y) * n_core + core) for d in range(1, n_y)]
    if n_core > 1:
        partners += [at(g=y * n_core + other)]

    w_copy = pltpu.make_async_copy(w_hbm, w_ref, w_sem)
    w_copy.start()
    barrier = pltpu.get_barrier_semaphore()
    for partner in partners:
        pl.semaphore_signal(barrier, inc=1, device_id=partner, device_id_type=MESH)
    pl.semaphore_wait(barrier, len(partners))

    def x_copy(d, piece):
        return pltpu.make_async_remote_copy(
            src_ref=x_ref.at[piece],
            dst_ref=x_all.at[d, piece],
            send_sem=xs_sem.at[d - 1, piece],
            recv_sem=xr_sem.at[d - 1, piece],
            device_id=at(t=(tp + n_tp - d) % n_tp),
            device_id_type=MESH,
        )

    for piece in range(pieces):
        for d in range(1, n_tp):
            x_copy(d, piece).start()

    def g_copy(way, hop, group):
        step = 1 if way == 0 else -1
        block = seq - step * hop
        return pltpu.make_async_remote_copy(
            src_ref=g_all.at[block, group],
            dst_ref=g_all.at[block, group],
            send_sem=gs_sem.at[way, hop, group],
            recv_sem=gr_sem.at[way, hop, group],
            device_id=at(s=seq + step),
            device_id_type=MESH,
        )

    def g_wait_copy(way, hop, group):
        step = 1 if way == 0 else -1
        block = seq - step * (hop + 1)
        return pltpu.make_async_remote_copy(
            src_ref=g_all.at[block, group],
            dst_ref=g_all.at[block, group],
            send_sem=gs_sem.at[way, hop, group],
            recv_sem=gr_sem.at[way, hop, group],
            device_id=at(s=seq - step),
            device_id_type=MESH,
        )

    def position(way):
        return seq if way == 0 else n_seq - 1 - seq

    def sends(way, hop):
        where = position(way)
        if hop == hops - 1:
            return where == n_seq - 2
        return (where >= hop) & (where <= n_seq - 3)

    def receives(way, hop):
        where = position(way)
        if hop == hops - 1:
            return where == n_seq - 1
        return (where >= hop + 1) & (where <= n_seq - 2)

    def picks_of(who):
        source = jnp.int32(0)
        live = jnp.int32(0)
        for rank in range(ids_ref.shape[1]):
            match = (ids_ref[0, rank] == who) & (rank < count_ref[0])
            source = jnp.where(match, slot_ref[0, rank], source)
            live = jnp.where(match, 1, live)
        return [jnp.where(source == block, live, 0).astype(F32) for block in range(n_seq)]

    end_picks = [picks_of(n_seq - 1), picks_of(0)]

    def pick_copy(way, group):
        step = 1 if way == 0 else -1
        return pltpu.make_async_remote_copy(
            src_ref=picked.at[way, group],
            dst_ref=g_all.at[seq, group],
            send_sem=gs_sem.at[way, hops - 1, group],
            recv_sem=gr_sem.at[way, hops - 1, group],
            device_id=at(s=seq + step),
            device_id_type=MESH,
        )

    def pick_wait_copy(way, group):
        step = 1 if way == 0 else -1
        return pltpu.make_async_remote_copy(
            src_ref=picked.at[way, group],
            dst_ref=g_all.at[seq - step, group],
            send_sem=gs_sem.at[way, hops - 1, group],
            recv_sem=gr_sem.at[way, hops - 1, group],
            device_id=at(s=seq - step),
            device_id_type=MESH,
        )

    def g_level(level):
        for way in range(2):

            @pl.when((level < groups) & sends(way, 0))
            def _():
                g_copy(way, 0, level).start()

        for hop in range(hops - 1, -1, -1):
            group = level - 1 - hop
            inside = (group >= 0) & (group < groups)
            for way in range(2):

                @pl.when(inside & receives(way, hop))
                def _():
                    if hop == hops - 1:
                        pick_wait_copy(way, group).wait_recv()
                    else:
                        g_wait_copy(way, hop, group).wait_recv()

                if hop + 1 < hops - 1:

                    @pl.when(inside & sends(way, hop + 1))
                    def _():
                        g_copy(way, hop + 1, group).start()

                if hop + 1 == hops - 1:

                    @pl.when(inside & sends(way, hop + 1))
                    def _():
                        blocks = range(n_seq - 1) if way == 0 else range(1, n_seq)
                        value = jnp.zeros((tokens, LANES), F32)
                        for block in blocks:
                            value = value + g_all[block, group].astype(F32) * end_picks[way][block]
                        picked[way, group] = value.astype(BF16)
                        pick_copy(way, group).start()

    for group in range(groups):
        g_all[seq, group] = g_ref[:, group * LANES : (group + 1) * LANES]
    for way in range(2):

        @pl.when(position(way) == n_seq - 1)
        def _():
            for block in range(n_seq - 2) if way == 0 else range(2, n_seq):
                g_all[block] = jnp.zeros(g_all.shape[1:], BF16)

    g_level(0)

    gain = gain_ref[...].astype(F32)
    aligned = piece_rows % 16 == 0

    def norm_piece(owner, piece, values):
        values = values.astype(F32)
        centred = values - jnp.mean(values, axis=-1, keepdims=True)
        spread = jnp.mean(centred * centred, axis=-1, keepdims=True)
        result = centred * lax.rsqrt(spread + 1e-05) * gain
        place = owner * pieces + piece
        if aligned:
            start = pl.multiple_of(place * piece_rows, 16)
            normed[pl.ds(start, piece_rows), :] = result.astype(BF16)
        else:
            normed32[place] = result

    for piece in range(pieces):
        norm_piece(tp, piece, x_ref[piece])
    for level in range(1, hops):
        g_level(level)
    w_copy.wait()

    def project(owner):
        rows = pl.ds(pl.multiple_of(owner * pieces * piece_rows, 16), pieces * piece_rows)
        for c in range(3):
            for group in range(groups):
                columns = slice(group * LANES, (group + 1) * LANES)
                result = mm(normed[rows, :], w_ref[c, :, columns], 1, 0)
                proj[c, group, rows, :] = result.astype(BF16)

    if aligned:
        project(tp)
    for piece in range(pieces):
        for d in range(1, n_tp):
            x_copy(d, piece).wait_recv()
            norm_piece((tp + d) % n_tp, piece, x_all[d, piece])
    if aligned:
        for d in range(1, n_tp):
            project((tp + d) % n_tp)
    else:
        normed[...] = normed32[...].reshape(tokens, width).astype(BF16)
        for c in range(3):
            for group in range(groups):
                columns = slice(group * LANES, (group + 1) * LANES)
                proj[c, group] = mm(normed[...], w_ref[c, :, columns], 1, 0).astype(BF16)
    normed_t[...] = normed[...].T

    picks = picks_of(seq)
    for block in range(n_seq):
        sent = ((seq == n_seq - 1) & (block == n_seq - 2)) | ((seq == 0) & (block == 1))
        picks[block] = jnp.where(sent, 1.0, picks[block])

    lane = lax.broadcasted_iota(jnp.int32, (1, LANES), 1)
    heads_here = LANES // HD
    masks = [
        ((lane >= h * HD) & (lane < (h + 1) * HD)).astype(F32).astype(BF16)
        for h in range(heads_here)
    ]

    def head(group, mask, cotangent):
        queries = proj[0, group]
        keys_own = proj[1, group] * mask
        values_own = proj[2, group] * mask
        scores = mm(keys_own, queries, 1, 1) * (HD**-0.5 * LOG2E)
        powers = jnp.exp2(scores - jnp.max(scores, axis=0, keepdims=True))
        attention = powers * (1.0 / jnp.sum(powers, axis=0, keepdims=True))
        grad_values = mm(attention.astype(BF16), cotangent * mask, 1, 0)
        grad_attention = mm(values_own, cotangent, 1, 1)
        weighted = attention * grad_attention
        inner = jnp.sum(weighted, axis=0, keepdims=True)
        scaled = ((weighted - attention * inner) * HD**-0.5).astype(BF16)
        grad_queries = mm(scaled, keys_own, 0, 0)
        grad_keys = mm(scaled, queries * mask, 1, 0)
        return grad_queries, grad_keys, grad_values

    def rows_of(who):
        return pl.ds(pl.multiple_of(who * block_rows, block_rows), block_rows)

    def copy1(group):
        return pltpu.make_async_remote_copy(
            src_ref=s1.at[group],
            dst_ref=r1.at[group],
            send_sem=s1_sem.at[group],
            recv_sem=r1_sem.at[group],
            device_id=at(g=y * n_core + other),
            device_id_type=MESH,
        )

    def owner_rows(e):
        place = (seq + e) % n_seq
        return pl.ds(pl.multiple_of(place * out_rows, out_rows), out_rows)

    def copy2(group, d, e):
        return pltpu.make_async_remote_copy(
            src_ref=s2.at[group, d - 1, owner_rows(e)],
            dst_ref=r2.at[group, d - 1, owner_rows(e)],
            send_sem=s2_sem.at[group, d - 1, e],
            recv_sem=r2_sem.at[group, d - 1, e],
            device_id=at(g=((y + d) % n_y) * n_core + core),
            device_id_type=MESH,
        )

    def copy3(group, d):
        return pltpu.make_async_remote_copy(
            src_ref=s3.at[group, d - 1],
            dst_ref=r3.at[group, d - 1],
            send_sem=s3_sem.at[group, d - 1],
            recv_sem=r3_sem.at[group, d - 1],
            device_id=at(s=(seq + d) % n_seq),
            device_id_type=MESH,
        )

    def reduce1(group):
        if n_core > 1:
            for place in range(n_y):
                s1[group, place] = total[group, rows_of(place * n_core + other), :].astype(BF16)
            copy1(group).start()

    def reduce2(group):
        if n_core > 1:
            copy1(group).wait_recv()

        def part(place):
            mine = total[group, rows_of(place * n_core + core), :]
            return mine + r1[group, place].astype(F32) if n_core > 1 else mine

        order = list(range(1, n_seq)) + [0]
        for d in range(1, n_y):
            s2[group, d - 1] = part((y + d) % n_y).astype(BF16)
            for e in order:
                copy2(group, d, e).start()
        acc[group] = part(y)

    def reduce3(group):
        def part(e):
            value = acc[group, owner_rows(e), :]
            for d in range(1, n_y):
                copy2(group, d, e).wait_recv()
                value = value + r2[group, d - 1, owner_rows(e), :].astype(F32)
            return value

        for e in range(1, n_seq):
            s3[group, e - 1] = part(e).astype(BF16)
            copy3(group, e).start()
        own[group] = part(0)

    def reduce4(group):
        value = own[group]
        for d in range(1, n_seq):
            copy3(group, d).wait_recv()
            value = value + r3[group, d - 1].astype(F32)
        return value

    def one_group(group, carry):
        g_level(hops + group)
        cotangent = g_all[0, group].astype(F32) * picks[0]
        for block in range(1, n_seq):
            cotangent = cotangent + g_all[block, group].astype(F32) * picks[block]
        cotangent = cotangent.astype(BF16)
        grads = head(group, masks[0], cotangent)

        @pl.when(group >= 1)
        def _():
            reduce2(group - 1)

        @pl.when(group >= 2)
        def _():
            reduce3(group - 2)

        for mask in masks[1:]:
            more = head(group, mask, cotangent)
            grads = [a + b for a, b in zip(grads, more)]

        joined = jnp.concatenate([grad.astype(BF16) for grad in grads], axis=1)
        product = mm(normed_t[...], joined, 1, 0)
        for c in range(3):
            total[group, c * width : (c + 1) * width, :] = product[:, c * LANES : (c + 1) * LANES]
        reduce1(group)
        return carry

    lax.fori_loop(0, groups, one_group, jnp.int32(0))
    reduce2(groups - 1)
    for group in range(max(groups - 2, 0), groups):
        reduce3(group)
    for group in range(groups):
        out_ref[:, group * LANES : (group + 1) * LANES] = reduce4(group)

    for piece in range(pieces):
        for d in range(1, n_tp):
            x_copy(d, piece).wait_send()
    for hop in range(hops):
        for way in range(2):

            @pl.when(sends(way, hop))
            def _():
                for group in range(groups):
                    copy = pick_copy(way, group) if hop == hops - 1 else g_copy(way, hop, group)
                    copy.wait_send()

    for group in range(groups):
        if n_core > 1:
            copy1(group).wait_send()
        for d in range(1, n_y):
            for e in range(n_seq):
                copy2(group, d, e).wait_send()
        for d in range(1, n_seq):
            copy3(group, d).wait_send()


def body(sizes, crops, dout, crop_count, crop_ids, seq_slot, norm_gain, qkv_weight):
    n_grp, n_tp, n_seq, n_core = sizes
    n_y = n_grp // n_core
    tok_local, width = crops.shape[2], crops.shape[3]
    tokens, cols = dout.shape[2], dout.shape[3]
    groups = cols // LANES
    out_rows = 3 * width // (n_grp * n_seq)
    block_rows = n_seq * out_rows
    pieces = 3 if tok_local % 48 == 0 else 1
    piece_rows = tok_local // pieces
    aligned = piece_rows % 16 == 0
    hops = n_seq - 1
    vmem = pl.BlockSpec(memory_space=pltpu.VMEM)
    smem = pl.BlockSpec(memory_space=pltpu.SMEM)
    dma = pltpu.SemaphoreType.DMA
    scratch = [
        pltpu.VMEM((3, width, cols), BF16),
        pltpu.VMEM((n_tp, pieces, piece_rows, width), BF16),
        pltpu.VMEM((8, LANES) if aligned else (n_tp * pieces, piece_rows, width), F32),
        pltpu.VMEM((tokens, width), BF16),
        pltpu.VMEM((width, tokens), BF16),
        pltpu.VMEM((3, groups, tokens, LANES), BF16),
        pltpu.VMEM((n_seq, groups, tokens, LANES), BF16),
        pltpu.VMEM((2, groups, tokens, LANES), BF16),
        pltpu.VMEM((groups, 3 * width, LANES), F32),
        pltpu.VMEM((groups, block_rows, LANES), F32),
        pltpu.VMEM((groups, out_rows, LANES), F32),
        pltpu.VMEM((groups, n_y, block_rows, LANES), BF16),
        pltpu.VMEM((groups, n_y, block_rows, LANES), BF16),
        pltpu.VMEM((groups, max(n_y - 1, 1), block_rows, LANES), BF16),
        pltpu.VMEM((groups, max(n_y - 1, 1), block_rows, LANES), BF16),
        pltpu.VMEM((groups, max(n_seq - 1, 1), out_rows, LANES), BF16),
        pltpu.VMEM((groups, max(n_seq - 1, 1), out_rows, LANES), BF16),
        dma,
        dma((max(n_tp - 1, 1), pieces)),
        dma((max(n_tp - 1, 1), pieces)),
        dma((2, hops, groups)),
        dma((2, hops, groups)),
        dma((groups,)),
        dma((groups,)),
        dma((groups, max(n_y - 1, 1), n_seq)),
        dma((groups, max(n_y - 1, 1), n_seq)),
        dma((groups, n_seq - 1)),
        dma((groups, n_seq - 1)),
    ]
    return pl.pallas_call(
        functools.partial(kernel, sizes),
        out_shape=jax.ShapeDtypeStruct((out_rows, cols), F32),
        in_specs=[vmem, vmem, smem, smem, smem, vmem, pl.BlockSpec(memory_space=pl.ANY)],
        out_specs=vmem,
        scratch_shapes=scratch,
        compiler_params=pltpu.CompilerParams(
            collective_id=0, has_side_effects=True, vmem_limit_bytes=56 * 2**20
        ),
        cost_estimate=pl.CostEstimate(
            flops=22 * tokens * width * cols, bytes_accessed=8 * width * cols, transcendentals=0
        ),
    )(
        crops.reshape(pieces, piece_rows, width),
        dout.reshape(tokens, cols),
        crop_count,
        crop_ids,
        seq_slot,
        norm_gain.reshape(1, width),
        qkv_weight,
    )


def solution(mesh):
    n_grp, n_tp, n_seq = mesh.shape["grp"], mesh.shape["tp"], mesh.shape["seq"]
    n_core = 2 if n_grp % 2 == 0 else 1
    in_specs = (
        P("grp", "seq", "tp", None),
        P("grp", "seq", None, "tp"),
        P("grp"),
        P("grp", None),
        P("grp", None),
        P(),
        P(None, None, "tp"),
    )
    out_specs = P(("grp", "seq"), "tp")
    return jax.shard_map(
        functools.partial(body, (n_grp, n_tp, n_seq, n_core)),
        mesh=mesh,
        in_specs=in_specs,
        out_specs=out_specs,
        check_vma=False,
    )
```
